32 devices in a mesh: groups: 2 (over y), row: 4 (over x, core), col: 4 (over z).
Axes of the slice: x: 2, y: 2, z: 4, core: 2. Of those that a mesh axis runs over, the one named last changes fastest.
Arguments:
- inputs: bfloat16 [256, 6144], P(('groups', 'row'), 'col'), parts along dimension 0, may hold values from -6 to 6
- upstream: bfloat16 [256, 6144], P(('groups', 'row'), 'col'), parts along dimension 0, may hold values from -6 to 6
- weight_in: bfloat16 [6144, 24576], P('col', 'row'), may hold values from -0.078125 to 0.078125
- weight_out: bfloat16 [24576, 6144], P('row', 'col'), may hold values from -0.0390625 to 0.0390625
Outputs:
- result: bfloat16 [256, 6144], P(('groups', 'row'), 'col'), parts along dimension 0
- grad_inputs: bfloat16 [256, 6144], P(('groups', 'row'), 'col'), parts along dimension 0
- grad_weight_in: bfloat16 [12288, 24576], P(('groups', 'col'), 'row'), parts along dimension 0
- grad_weight_out: bfloat16 [49152, 6144], P(('groups', 'row'), 'col'), parts along dimension 0
The draws below stay inside these ranges and needn't reach their ends.
There are 2 independent parts, one for each index of `groups`. The reference program is written for one: setup_inputs(seed, part) draws one part's arguments, and reference() takes and returns one part's arrays. A program takes and returns all parts, laid end to end along the dimension named above; an argument that names none is the same for every part. Nothing has to cross between parts.
All inputs are finite; a program needn't handle non-finite values.
Results may differ from the reference program's by a relative error of at most 0.0051.
Values may be sent and summed in bfloat16 or wider, within the bound.
A program may use at most 192 MiB of HBM per device.

```python
import math
import jax
import jax.numpy as jnp
from jax import lax

D = 6144
FF = 24576
TOKENS = 128


def steps_of(rng, dims, shards, smallest, largest):
    def one(position, parts):
        heights = jax.random.uniform(jax.random.fold_in(jax.random.fold_in(rng, 6), position), (parts,), jnp.float32, smallest / len(shards), largest / len(shards))
        return jnp.repeat(jnp.exp(heights), dims[position] // parts).reshape((-1,) + (1,) * (len(dims) - position - 1))

    loudness = one(*shards[0])
    for cut in shards[1:]:
        loudness = loudness * one(*cut)
    return loudness


def noise(key, shape, deviation, bound, split=(), kind=jnp.bfloat16):
    values = deviation * jax.random.normal(key, shape, jnp.float32)
    if split:
        values = values * steps_of(key, shape, split, -0.22, 0.18)
    return jnp.clip(values, -bound, bound).astype(kind)


def setup_inputs(seed: int = 0, part: int = 0) -> dict:
    arg_keys = jax.random.split(jax.random.key(seed), 5)
    part_splits = jax.random.split(jax.random.fold_in(arg_keys[4], part), 5)
    return {
        "inputs": noise(part_splits[0], (TOKENS, D), 1.0, 6.0, ((0, 4), (1, 4))),
        "upstream": noise(part_splits[1], (TOKENS, D), 1.0, 6.0, ((0, 4), (1, 4))),
        "weight_in": noise(arg_keys[2], (D, FF), D ** -0.5, 0.078125, ((0, 4), (1, 4))),
        "weight_out": noise(arg_keys[3], (FF, D), FF ** -0.5, 0.0390625, ((0, 4), (1, 4))),
    }


gelu_c = math.sqrt(2.0 / math.pi)

def gelu_parts(preact):
    inner = gelu_c * (preact + 0.044715 * preact * preact * preact)
    tangent = jnp.tanh(inner)
    value = 0.5 * preact * (1.0 + tangent)
    slope = 0.5 * (1.0 + tangent) + 0.5 * preact * (1.0 - tangent * tangent) * gelu_c * (1.0 + 3.0 * 0.044715 * preact * preact)
    return (value, slope)

def reference(inputs, upstream, weight_in, weight_out):
    preact = jnp.dot(inputs, weight_in, preferred_element_type=jnp.float32)
    value, slope = gelu_parts(preact)
    activation = value.astype(jnp.bfloat16)
    result = jnp.dot(activation, weight_out, preferred_element_type=jnp.float32).astype(jnp.bfloat16)
    grad_act = lax.dot_general(upstream, weight_out, (((1,), (1,)), ((), ())), preferred_element_type=jnp.float32)
    grad_pre = (grad_act * slope).astype(jnp.bfloat16)
    grad_inputs = lax.dot_general(grad_pre, weight_in, (((1,), (1,)), ((), ())), preferred_element_type=jnp.float32).astype(jnp.bfloat16)
    grad_weight_in = lax.dot_general(inputs, grad_pre, (((0,), (0,)), ((), ())), preferred_element_type=jnp.float32).astype(jnp.bfloat16)
    grad_weight_out = lax.dot_general(activation, upstream, (((0,), (0,)), ((), ())), preferred_element_type=jnp.float32).astype(jnp.bfloat16)
    return (result, grad_inputs, grad_weight_in, grad_weight_out)
```

```python
import functools
import math

import jax
import jax.numpy as jnp
from jax import lax
from jax.experimental import pallas as pl
from jax.experimental.pallas import tpu as pltpu
from jax.sharding import PartitionSpec as P

gelu_c = math.sqrt(2.0 / math.pi)
MESH = pl.DeviceIdType.MESH
CHUNK = 256
RING = 8
RELAY, OWN, SPREAD = 1, 3, 6
NT = (((1,), (1,)), ((), ()))
TN = (((0,), (0,)), ((), ()))


def local_gelu(preact, grad_act):
    inner = gelu_c * (preact + 0.044715 * preact * preact * preact)
    tangent = jnp.tanh(inner)
    value = 0.5 * preact * (1.0 + tangent)
    slope = 0.5 * (1.0 + tangent) + 0.5 * preact * (1.0 - tangent * tangent) * gelu_c * (
        1.0 + 3.0 * 0.044715 * preact * preact
    )
    return (value.astype(jnp.bfloat16), (grad_act * slope).astype(jnp.bfloat16))


def block_kernel(
    n_row, n_col, chunks,
    x_ref, dy_ref, win_hbm, wout_hbm,
    acts_hbm, xall_hbm, dyall_hbm, out_ref, back_ref,
    xall, dyall, win, wout, local, outgoing, from_left, from_right, acts,
    w_sem, g_send, g_recv, rs_send, left_recv, right_recv, ag_send, ag_recv, save_sem, tok_sem,
):
    row, col = lax.axis_index("row"), lax.axis_index("col")
    own = x_ref.shape[0]
    tokens = own * n_row
    pair, core = row // 2, row % 2
    pairs = n_row // 2
    sibling = pair * 2 + 1 - core
    mid = n_col // 2
    has_left = col > 0
    has_right = col < n_col - 1
    edge = jnp.logical_or(col == 0, col == n_col - 1)
    depth = x_ref.shape[1]

    def weight_copies(k):
        at = pl.ds(pl.multiple_of(k * CHUNK, CHUNK), CHUNK)
        return (
            pltpu.make_async_copy(win_hbm.at[:, at], win.at[k], w_sem.at[0, k]),
            pltpu.make_async_copy(wout_hbm.at[at, :], wout.at[k], w_sem.at[1, k]),
        )

    def load(k, carry):
        for copy in weight_copies(k):
            copy.start()
        return carry

    lax.fori_loop(0, chunks, load, 0)

    barrier = pltpu.get_barrier_semaphore()
    pl.semaphore_signal(barrier, inc=1, device_id={"row": sibling}, device_id_type=MESH)
    for o in range(1, pairs):
        peer = lax.rem(pair + o, pairs) * 2 + core
        pl.semaphore_signal(barrier, inc=1, device_id={"row": peer}, device_id_type=MESH)

    @pl.when(has_left)
    def _():
        pl.semaphore_signal(barrier, inc=1, device_id={"col": col - 1}, device_id_type=MESH)

    @pl.when(has_right)
    def _():
        pl.semaphore_signal(barrier, inc=1, device_id={"col": col + 1}, device_id_type=MESH)

    pl.semaphore_wait(barrier, pairs + jnp.where(edge, 1, 2))

    def token_copy(which, block, slot, peer, mine):
        ref, all_ref = ((x_ref, xall), (dy_ref, dyall))[which]
        at = pl.ds(pl.multiple_of(block * own, own), own)
        return pltpu.make_async_remote_copy(
            src_ref=ref if mine else all_ref.at[at],
            dst_ref=all_ref.at[at],
            send_sem=g_send.at[which, slot],
            recv_sem=g_recv.at[which, block],
            device_id={"row": peer},
            device_id_type=MESH,
        )

    sends = []
    for which in range(2):
        for o in range(1, pairs):
            sends.append(token_copy(which, row, o, lax.rem(pair + o, pairs) * 2 + core, True))
            sends[-1].start()
        sends.append(token_copy(which, row, 0, sibling, True))
        sends[-1].start()
    mine = pl.ds(pl.multiple_of(row * own, own), own)
    xall[mine, :] = x_ref[...]
    dyall[mine, :] = dy_ref[...]
    out_ref[...] = jnp.zeros_like(out_ref)
    back_ref[...] = jnp.zeros_like(back_ref)
    for which in range(2):
        for o in range(1, pairs):
            block = lax.rem(pair + pairs - o, pairs) * 2 + core
            onward = token_copy(which, block, pairs + o - 1, sibling, False)
            onward.wait_recv()
            onward.start()
            sends.append(onward)
    for which in range(2):
        for q in range(pairs):
            token_copy(which, q * 2 + 1 - core, 0, sibling, False).wait_recv()
    for copy in sends:
        copy.wait_send()
    keep = (
        pltpu.make_async_copy(xall, xall_hbm, tok_sem.at[0]),
        pltpu.make_async_copy(dyall, dyall_hbm, tok_sem.at[1]),
    )
    for copy in keep:
        copy.start()

    def owner(k):
        return mid - 1 + lax.rem(k, 2)

    def sum_right(k):
        return pltpu.make_async_remote_copy(
            src_ref=outgoing.at[k], dst_ref=from_left.at[k],
            send_sem=rs_send.at[k], recv_sem=left_recv.at[k],
            device_id={"col": col + 1}, device_id_type=MESH,
        )

    def sum_left(k):
        return pltpu.make_async_remote_copy(
            src_ref=outgoing.at[k], dst_ref=from_right.at[k],
            send_sem=rs_send.at[k], recv_sem=right_recv.at[k],
            device_id={"col": col - 1}, device_id_type=MESH,
        )

    def spread(k, side):
        return pltpu.make_async_remote_copy(
            src_ref=acts.at[k], dst_ref=acts.at[k],
            send_sem=ag_send.at[side, k], recv_sem=ag_recv.at[k],
            device_id={"col": col - 1 + 2 * side}, device_id_type=MESH,
        )

    def save(k):
        return pltpu.make_async_copy(acts.at[k], acts_hbm.at[k], save_sem.at[k])

    def multiply(k):
        for copy in weight_copies(k):
            copy.wait()
        slot = lax.rem(k, RING)
        pre = jnp.dot(xall[...], win[k], preferred_element_type=jnp.float32)
        grad = lax.dot_general(dyall[...], wout[k], NT, preferred_element_type=jnp.float32)

        @pl.when(edge)
        def _():
            outgoing[k, :tokens, :] = pre.astype(jnp.bfloat16)
            outgoing[k, tokens:, :] = grad.astype(jnp.bfloat16)

        @pl.when(jnp.logical_not(edge))
        def _():
            local[slot, :tokens, :] = pre
            local[slot, tokens:, :] = grad

        @pl.when(col == 0)
        def _():
            sum_right(k).start()

        @pl.when(col == n_col - 1)
        def _():
            sum_left(k).start()

    def relay(k):
        slot = lax.rem(k, RING)

        @pl.when(jnp.logical_and(has_left, col < owner(k)))
        def _():
            copy = sum_right(k)
            copy.wait_recv()
            outgoing[k] = (local[slot] + from_left[k].astype(jnp.float32)).astype(jnp.bfloat16)
            copy.start()

        @pl.when(jnp.logical_and(has_right, col > owner(k)))
        def _():
            copy = sum_left(k)
            copy.wait_recv()
            outgoing[k] = (local[slot] + from_right[k].astype(jnp.float32)).astype(jnp.bfloat16)
            copy.start()

    def activate(k):
        slot = lax.rem(k, RING)

        @pl.when(col == owner(k))
        def _():
            sum_right(k).wait_recv()
            sum_left(k).wait_recv()
            total = (
                local[slot] + from_left[k].astype(jnp.float32) + from_right[k].astype(jnp.float32)
            )
            value, slope = local_gelu(total[:tokens], total[tokens:])
            acts[k, :tokens, :] = value
            acts[k, tokens:, :] = slope
            spread(k, 0).start()
            spread(k, 1).start()

    def finish(k):
        @pl.when(col < owner(k))
        def _():
            copy = spread(k, 0)
            copy.wait_recv()

            @pl.when(has_left)
            def _():
                copy.start()

        @pl.when(col > owner(k))
        def _():
            copy = spread(k, 1)
            copy.wait_recv()

            @pl.when(has_right)
            def _():
                copy.start()

        save(k).start()
        out_ref[...] += jnp.dot(acts[k, :tokens, :], wout[k], preferred_element_type=jnp.float32)
        back_ref[...] += lax.dot_general(
            acts[k, tokens:, :], win[k], NT, preferred_element_type=jnp.float32
        )

    def step(s, carry):
        for trail, stage in ((0, multiply), (RELAY, relay), (OWN, activate), (SPREAD, finish)):
            @pl.when(jnp.logical_and(s >= trail, s < chunks + trail))
            def _():
                stage(s - trail)
        return carry

    lax.fori_loop(0, chunks + SPREAD, step, 0)

    def drain(k, carry):
        @pl.when(col < owner(k))
        def _():
            sum_right(k).wait_send()

        @pl.when(col > owner(k))
        def _():
            sum_left(k).wait_send()

        @pl.when(jnp.logical_and(has_left, col <= owner(k)))
        def _():
            spread(k, 0).wait_send()

        @pl.when(jnp.logical_and(has_right, col >= owner(k)))
        def _():
            spread(k, 1).wait_send()

        save(k).wait()
        return carry

    lax.fori_loop(0, chunks, drain, 0)
    for copy in keep:
        copy.wait()


def run_block(n_row, n_col, x, dy, w_in, w_out):
    own, depth = x.shape
    hidden = w_in.shape[1]
    chunks = hidden // CHUNK
    tokens = own * n_row
    bf, f32 = jnp.bfloat16, jnp.float32
    vmem = pl.BlockSpec(memory_space=pltpu.VMEM)
    anywhere = pl.BlockSpec(memory_space=pl.ANY)
    dma = pltpu.SemaphoreType.DMA
    stack = (chunks, 2 * tokens, CHUNK)
    return pl.pallas_call(
        functools.partial(block_kernel, n_row, n_col, chunks),
        out_shape=(
            jax.ShapeDtypeStruct(stack, bf),
            jax.ShapeDtypeStruct((tokens, depth), bf),
            jax.ShapeDtypeStruct((tokens, depth), bf),
            jax.ShapeDtypeStruct((tokens, depth), f32),
            jax.ShapeDtypeStruct((tokens, depth), f32),
        ),
        in_specs=[vmem, vmem, anywhere, anywhere],
        out_specs=(anywhere, anywhere, anywhere, vmem, vmem),
        scratch_shapes=[
            pltpu.VMEM((tokens, depth), bf),
            pltpu.VMEM((tokens, depth), bf),
            pltpu.VMEM((chunks, depth, CHUNK), bf),
            pltpu.VMEM((chunks, CHUNK, depth), bf),
            pltpu.VMEM((RING, 2 * tokens, CHUNK), f32),
            pltpu.VMEM(stack, bf),
            pltpu.VMEM(stack, bf),
            pltpu.VMEM(stack, bf),
            pltpu.VMEM(stack, bf),
            dma((2, chunks)),
            dma((2, n_row)),
            dma((2, n_row)),
            dma((chunks,)),
            dma((chunks,)),
            dma((chunks,)),
            dma((2, chunks)),
            dma((chunks,)),
            dma((chunks,)),
            dma((2,)),
        ],
        compiler_params=pltpu.CompilerParams(
            collective_id=0, has_side_effects=True, vmem_limit_bytes=60 * 2**20
        ),
        cost_estimate=pl.CostEstimate(
            flops=8 * tokens * depth * hidden,
            bytes_accessed=4 * depth * hidden,
            transcendentals=tokens * hidden,
        ),
        name="block",
    )(x, dy, w_in, w_out)


def grads_kernel(x_ref, dy_ref, acts_ref, gin_ref, gout_ref, xt):
    tokens = x_ref.shape[0]

    @pl.when(pl.program_id(0) == 0)
    def _():
        xt[...] = x_ref[...].T

    for i in range(acts_ref.shape[0]):
        at = slice(i * CHUNK, (i + 1) * CHUNK)
        gin_ref[:, at] = jnp.dot(
            xt[...], acts_ref[i, tokens:, :], preferred_element_type=jnp.float32
        ).astype(jnp.bfloat16)
        gout_ref[at, :] = lax.dot_general(
            acts_ref[i, :tokens, :], dy_ref[...], TN, preferred_element_type=jnp.float32
        ).astype(jnp.bfloat16)


def weight_grads(x, dy, acts):
    tokens, depth = x.shape
    chunks = acts.shape[0]
    hidden = chunks * CHUNK
    per = 2
    bf = jnp.bfloat16
    return pl.pallas_call(
        grads_kernel,
        grid=(chunks // per,),
        out_shape=(
            jax.ShapeDtypeStruct((depth, hidden), bf),
            jax.ShapeDtypeStruct((hidden, depth), bf),
        ),
        in_specs=[
            pl.BlockSpec((tokens, depth), lambda s: (0, 0)),
            pl.BlockSpec((tokens, depth), lambda s: (0, 0)),
            pl.BlockSpec((per, 2 * tokens, CHUNK), lambda s: (s, 0, 0)),
        ],
        out_specs=(
            pl.BlockSpec((depth, per * CHUNK), lambda s: (0, s)),
            pl.BlockSpec((per * CHUNK, depth), lambda s: (s, 0)),
        ),
        scratch_shapes=[pltpu.VMEM((depth, tokens), bf)],
        compiler_params=pltpu.CompilerParams(vmem_limit_bytes=40 * 2**20),
        cost_estimate=pl.CostEstimate(
            flops=4 * tokens * depth * hidden,
            bytes_accessed=4 * depth * hidden,
            transcendentals=0,
        ),
        name="grads",
    )(x, dy, acts)


def shards(n_row, n_col, inputs, upstream, weight_in, weight_out):
    acts, x_all, dy_all, part_out, part_back = run_block(
        n_row, n_col, inputs, upstream, weight_in, weight_out
    )
    summed_out, summed_back = (
        lax.psum_scatter(part_out, "row", scatter_dimension=0, tiled=True),
        lax.psum_scatter(part_back, "row", scatter_dimension=0, tiled=True),
    )
    grad_weight_in, grad_weight_out = weight_grads(x_all, dy_all, acts)
    return (
        summed_out.astype(jnp.bfloat16),
        summed_back.astype(jnp.bfloat16),
        grad_weight_in,
        grad_weight_out,
    )


def solution(mesh):
    placed = (
        P(("groups", "row"), "col"),
        P(("groups", "row"), "col"),
        P("col", "row"),
        P("row", "col"),
    )
    return jax.shard_map(
        functools.partial(shards, mesh.shape["row"], mesh.shape["col"]),
        mesh=mesh,
        in_specs=placed,
        out_specs=(
            P(("groups", "row"), "col"),
            P(("groups", "row"), "col"),
            P(("groups", "col"), "row"),
            P(("groups", "row"), "col"),
        ),
        check_vma=False,
    )
```

```python
import functools
import math

import jax
import jax.numpy as jnp
from jax import lax
from jax.experimental import pallas as pl
from jax.experimental.pallas import tpu as pltpu
from jax.sharding import PartitionSpec as P

gelu_c = math.sqrt(2.0 / math.pi)
MESH = pl.DeviceIdType.MESH
CHUNK = 256
RING = 8
RELAY, OWN, SPREAD = 1, 3, 6
NT = (((1,), (1,)), ((), ()))
TN = (((0,), (0,)), ((), ()))


def local_gelu(preact, grad_act):
    inner = gelu_c * (preact + 0.044715 * preact * preact * preact)
    tangent = jnp.tanh(inner)
    value = 0.5 * preact * (1.0 + tangent)
    slope = 0.5 * (1.0 + tangent) + 0.5 * preact * (1.0 - tangent * tangent) * gelu_c * (
        1.0 + 3.0 * 0.044715 * preact * preact
    )
    return (value.astype(jnp.bfloat16), (grad_act * slope).astype(jnp.bfloat16))


def block_kernel(
    n_row, n_col, chunks,
    x_ref, dy_ref, win_hbm, wout_hbm,
    acts_hbm, xall_hbm, dyall_hbm, result_ref, gin_ref,
    sums, core_in, chip_out, chip_in, xall, dyall, win, wout, local, outgoing, from_left, from_right, acts,
    w_sem, g_send, g_recv, rs_send, left_recv, right_recv, ag_send, ag_recv, save_sem, tok_sem,
    core_send, core_recv, chip_send, chip_recv,
):
    row, col = lax.axis_index("row"), lax.axis_index("col")
    own = x_ref.shape[0]
    tokens = own * n_row
    pair, core = row // 2, row % 2
    pairs = n_row // 2
    sibling = pair * 2 + 1 - core
    mid = n_col // 2
    has_left = col > 0
    has_right = col < n_col - 1
    edge = jnp.logical_or(col == 0, col == n_col - 1)
    depth = x_ref.shape[1]

    def weight_copies(k):
        at = pl.ds(pl.multiple_of(k * CHUNK, CHUNK), CHUNK)
        return (
            pltpu.make_async_copy(win_hbm.at[:, at], win.at[k], w_sem.at[0, k]),
            pltpu.make_async_copy(wout_hbm.at[at, :], wout.at[k], w_sem.at[1, k]),
        )

    def load(k, carry):
        for copy in weight_copies(k):
            copy.start()
        return carry

    lax.fori_loop(0, chunks, load, 0)

    barrier = pltpu.get_barrier_semaphore()
    pl.semaphore_signal(barrier, inc=1, device_id={"row": sibling}, device_id_type=MESH)
    for o in range(1, pairs):
        peer = lax.rem(pair + o, pairs) * 2 + core
        pl.semaphore_signal(barrier, inc=1, device_id={"row": peer}, device_id_type=MESH)

    @pl.when(has_left)
    def _():
        pl.semaphore_signal(barrier, inc=1, device_id={"col": col - 1}, device_id_type=MESH)

    @pl.when(has_right)
    def _():
        pl.semaphore_signal(barrier, inc=1, device_id={"col": col + 1}, device_id_type=MESH)

    pl.semaphore_wait(barrier, pairs + jnp.where(edge, 1, 2))

    def token_copy(which, block, slot, peer, mine):
        ref, all_ref = ((x_ref, xall), (dy_ref, dyall))[which]
        at = pl.ds(pl.multiple_of(block * own, own), own)
        return pltpu.make_async_remote_copy(
            src_ref=ref if mine else all_ref.at[at],
            dst_ref=all_ref.at[at],
            send_sem=g_send.at[which, slot],
            recv_sem=g_recv.at[which, block],
            device_id={"row": peer},
            device_id_type=MESH,
        )

    sends = []
    for which in range(2):
        for o in range(1, pairs):
            sends.append(token_copy(which, row, o, lax.rem(pair + o, pairs) * 2 + core, True))
            sends[-1].start()
        sends.append(token_copy(which, row, 0, sibling, True))
        sends[-1].start()
    mine = pl.ds(pl.multiple_of(row * own, own), own)
    xall[mine, :] = x_ref[...]
    dyall[mine, :] = dy_ref[...]
    sums[...] = jnp.zeros_like(sums)
    for which in range(2):
        for o in range(1, pairs):
            block = lax.rem(pair + pairs - o, pairs) * 2 + core
            onward = token_copy(which, block, pairs + o - 1, sibling, False)
            onward.wait_recv()
            onward.start()
            sends.append(onward)
    for which in range(2):
        for q in range(pairs):
            token_copy(which, q * 2 + 1 - core, 0, sibling, False).wait_recv()
    for copy in sends:
        copy.wait_send()
    keep = (
        pltpu.make_async_copy(xall, xall_hbm, tok_sem.at[0]),
        pltpu.make_async_copy(dyall, dyall_hbm, tok_sem.at[1]),
    )
    for copy in keep:
        copy.start()

    def owner(k):
        return mid - 1 + lax.rem(k, 2)

    def sum_right(k):
        return pltpu.make_async_remote_copy(
            src_ref=outgoing.at[k], dst_ref=from_left.at[k],
            send_sem=rs_send.at[k], recv_sem=left_recv.at[k],
            device_id={"col": col + 1}, device_id_type=MESH,
        )

    def sum_left(k):
        return pltpu.make_async_remote_copy(
            src_ref=outgoing.at[k], dst_ref=from_right.at[k],
            send_sem=rs_send.at[k], recv_sem=right_recv.at[k],
            device_id={"col": col - 1}, device_id_type=MESH,
        )

    def spread(k, side):
        return pltpu.make_async_remote_copy(
            src_ref=acts.at[k], dst_ref=acts.at[k],
            send_sem=ag_send.at[side, k], recv_sem=ag_recv.at[k],
            device_id={"col": col - 1 + 2 * side}, device_id_type=MESH,
        )

    def save(k):
        return pltpu.make_async_copy(acts.at[k], acts_hbm.at[k], save_sem.at[k])

    def multiply(k):
        for copy in weight_copies(k):
            copy.wait()
        slot = lax.rem(k, RING)
        pre = jnp.dot(xall[...], win[k], preferred_element_type=jnp.float32)
        grad = lax.dot_general(dyall[...], wout[k], NT, preferred_element_type=jnp.float32)

        @pl.when(edge)
        def _():
            outgoing[k, :tokens, :] = pre.astype(jnp.bfloat16)
            outgoing[k, tokens:, :] = grad.astype(jnp.bfloat16)

        @pl.when(jnp.logical_not(edge))
        def _():
            local[slot, :tokens, :] = pre
            local[slot, tokens:, :] = grad

        @pl.when(col == 0)
        def _():
            sum_right(k).start()

        @pl.when(col == n_col - 1)
        def _():
            sum_left(k).start()

    def relay(k):
        slot = lax.rem(k, RING)

        @pl.when(jnp.logical_and(has_left, col < owner(k)))
        def _():
            copy = sum_right(k)
            copy.wait_recv()
            outgoing[k] = (local[slot] + from_left[k].astype(jnp.float32)).astype(jnp.bfloat16)
            copy.start()

        @pl.when(jnp.logical_and(has_right, col > owner(k)))
        def _():
            copy = sum_left(k)
            copy.wait_recv()
            outgoing[k] = (local[slot] + from_right[k].astype(jnp.float32)).astype(jnp.bfloat16)
            copy.start()

    def activate(k):
        slot = lax.rem(k, RING)

        @pl.when(col == owner(k))
        def _():
            sum_right(k).wait_recv()
            sum_left(k).wait_recv()
            total = (
                local[slot] + from_left[k].astype(jnp.float32) + from_right[k].astype(jnp.float32)
            )
            value, slope = local_gelu(total[:tokens], total[tokens:])
            acts[k, :tokens, :] = value
            acts[k, tokens:, :] = slope
            spread(k, 0).start()
            spread(k, 1).start()

    def finish(k):
        @pl.when(col < owner(k))
        def _():
            copy = spread(k, 0)
            copy.wait_recv()

            @pl.when(has_left)
            def _():
                copy.start()

        @pl.when(col > owner(k))
        def _():
            copy = spread(k, 1)
            copy.wait_recv()

            @pl.when(has_right)
            def _():
                copy.start()

        save(k).start()
        sums[0] += jnp.dot(acts[k, :tokens, :], wout[k], preferred_element_type=jnp.float32)
        sums[1] += lax.dot_general(
            acts[k, tokens:, :], win[k], NT, preferred_element_type=jnp.float32
        )

    def step(s, carry):
        for trail, stage in ((0, multiply), (RELAY, relay), (OWN, activate), (SPREAD, finish)):
            @pl.when(jnp.logical_and(s >= trail, s < chunks + trail))
            def _():
                stage(s - trail)
        return carry

    lax.fori_loop(0, chunks + SPREAD, step, 0)

    def rows_of(block):
        return pl.ds(pl.multiple_of(block * own, own), own)

    def to_core(which, o):
        block = lax.rem(pair + o, pairs) * 2 + 1 - core
        return pltpu.make_async_remote_copy(
            src_ref=sums.at[which, rows_of(block)], dst_ref=core_in.at[which, o],
            send_sem=core_send.at[which, o], recv_sem=core_recv.at[which, o],
            device_id={"row": sibling}, device_id_type=MESH,
        )

    def to_chip(which, o):
        return pltpu.make_async_remote_copy(
            src_ref=chip_out.at[which, o], dst_ref=chip_in.at[which, o],
            send_sem=chip_send.at[which, o], recv_sem=chip_recv.at[which, o],
            device_id={"row": lax.rem(pair + o, pairs) * 2 + core}, device_id_type=MESH,
        )

    order = list(range(1, pairs)) + [0]
    for o in order:
        for which in range(2):
            to_core(which, o).start()
    for o in order[:-1]:
        block = lax.rem(pair + o, pairs) * 2 + core
        for which in range(2):
            to_core(which, o).wait_recv()
            chip_out[which, o] = (sums[which, rows_of(block), :] + core_in[which, o]).astype(
                jnp.bfloat16
            )
            to_chip(which, o).start()

    def drain(k, carry):
        @pl.when(col < owner(k))
        def _():
            sum_right(k).wait_send()

        @pl.when(col > owner(k))
        def _():
            sum_left(k).wait_send()

        @pl.when(jnp.logical_and(has_left, col <= owner(k)))
        def _():
            spread(k, 0).wait_send()

        @pl.when(jnp.logical_and(has_right, col >= owner(k)))
        def _():
            spread(k, 1).wait_send()

        save(k).wait()
        return carry

    lax.fori_loop(0, chunks, drain, 0)
    for copy in keep:
        copy.wait()
    for which, ref in ((0, result_ref), (1, gin_ref)):
        to_core(which, 0).wait_recv()
        total = sums[which, rows_of(row), :] + core_in[which, 0]
        for o in range(1, pairs):
            to_chip(which, o).wait_recv()
            total += chip_in[which, o].astype(jnp.float32)
        ref[...] = total.astype(jnp.bfloat16)
    for which in range(2):
        for o in order:
            to_core(which, o).wait_send()
        for o in order[:-1]:
            to_chip(which, o).wait_send()


def run_block(n_row, n_col, x, dy, w_in, w_out):
    own, depth = x.shape
    hidden = w_in.shape[1]
    chunks = hidden // CHUNK
    tokens = own * n_row
    bf, f32 = jnp.bfloat16, jnp.float32
    vmem = pl.BlockSpec(memory_space=pltpu.VMEM)
    anywhere = pl.BlockSpec(memory_space=pl.ANY)
    dma = pltpu.SemaphoreType.DMA
    stack = (chunks, 2 * tokens, CHUNK)
    return pl.pallas_call(
        functools.partial(block_kernel, n_row, n_col, chunks),
        out_shape=(
            jax.ShapeDtypeStruct(stack, bf),
            jax.ShapeDtypeStruct((tokens, depth), bf),
            jax.ShapeDtypeStruct((tokens, depth), bf),
            jax.ShapeDtypeStruct((own, depth), bf),
            jax.ShapeDtypeStruct((own, depth), bf),
        ),
        in_specs=[vmem, vmem, anywhere, anywhere],
        out_specs=(anywhere, anywhere, anywhere, vmem, vmem),
        scratch_shapes=[
            pltpu.VMEM((2, tokens, depth), f32),
            pltpu.VMEM((2, n_row // 2, own, depth), f32),
            pltpu.VMEM((2, n_row // 2, own, depth), bf),
            pltpu.VMEM((2, n_row // 2, own, depth), bf),
            pltpu.VMEM((tokens, depth), bf),
            pltpu.VMEM((tokens, depth), bf),
            pltpu.VMEM((chunks, depth, CHUNK), bf),
            pltpu.VMEM((chunks, CHUNK, depth), bf),
            pltpu.VMEM((RING, 2 * tokens, CHUNK), f32),
            pltpu.VMEM(stack, bf),
            pltpu.VMEM(stack, bf),
            pltpu.VMEM(stack, bf),
            pltpu.VMEM(stack, bf),
            dma((2, chunks)),
            dma((2, n_row)),
            dma((2, n_row)),
            dma((chunks,)),
            dma((chunks,)),
            dma((chunks,)),
            dma((2, chunks)),
            dma((chunks,)),
            dma((chunks,)),
            dma((2,)),
            dma((2, n_row // 2)),
            dma((2, n_row // 2)),
            dma((2, n_row // 2)),
            dma((2, n_row // 2)),
        ],
        compiler_params=pltpu.CompilerParams(
            collective_id=0, has_side_effects=True, vmem_limit_bytes=60 * 2**20
        ),
        cost_estimate=pl.CostEstimate(
            flops=8 * tokens * depth * hidden,
            bytes_accessed=4 * depth * hidden,
            transcendentals=tokens * hidden,
        ),
        name="block",
    )(x, dy, w_in, w_out)


def grads_kernel(x_ref, dy_ref, acts_ref, gin_ref, gout_ref, xt):
    tokens = x_ref.shape[0]

    @pl.when(pl.program_id(0) == 0)
    def _():
        xt[...] = x_ref[...].T

    for i in range(acts_ref.shape[0]):
        at = slice(i * CHUNK, (i + 1) * CHUNK)
        gin_ref[:, at] = jnp.dot(
            xt[...], acts_ref[i, tokens:, :], preferred_element_type=jnp.float32
        ).astype(jnp.bfloat16)
        gout_ref[at, :] = lax.dot_general(
            acts_ref[i, :tokens, :], dy_ref[...], TN, preferred_element_type=jnp.float32
        ).astype(jnp.bfloat16)


def weight_grads(x, dy, acts):
    tokens, depth = x.shape
    chunks = acts.shape[0]
    hidden = chunks * CHUNK
    per = 2
    bf = jnp.bfloat16
    return pl.pallas_call(
        grads_kernel,
        grid=(chunks // per,),
        out_shape=(
            jax.ShapeDtypeStruct((depth, hidden), bf),
            jax.ShapeDtypeStruct((hidden, depth), bf),
        ),
        in_specs=[
            pl.BlockSpec((tokens, depth), lambda s: (0, 0)),
            pl.BlockSpec((tokens, depth), lambda s: (0, 0)),
            pl.BlockSpec((per, 2 * tokens, CHUNK), lambda s: (s, 0, 0)),
        ],
        out_specs=(
            pl.BlockSpec((depth, per * CHUNK), lambda s: (0, s)),
            pl.BlockSpec((per * CHUNK, depth), lambda s: (s, 0)),
        ),
        scratch_shapes=[pltpu.VMEM((depth, tokens), bf)],
        compiler_params=pltpu.CompilerParams(vmem_limit_bytes=60 * 2**20),
        cost_estimate=pl.CostEstimate(
            flops=4 * tokens * depth * hidden,
            bytes_accessed=4 * depth * hidden,
            transcendentals=0,
        ),
        name="grads",
    )(x, dy, acts)


def shards(n_row, n_col, inputs, upstream, weight_in, weight_out):
    acts, x_all, dy_all, result, grad_inputs = run_block(
        n_row, n_col, inputs, upstream, weight_in, weight_out
    )
    grad_weight_in, grad_weight_out = weight_grads(x_all, dy_all, acts)
    return result, grad_inputs, grad_weight_in, grad_weight_out


def solution(mesh):
    placed = (
        P(("groups", "row"), "col"),
        P(("groups", "row"), "col"),
        P("col", "row"),
        P("row", "col"),
    )
    return jax.shard_map(
        functools.partial(shards, mesh.shape["row"], mesh.shape["col"]),
        mesh=mesh,
        in_specs=placed,
        out_specs=(
            P(("groups", "row"), "col"),
            P(("groups", "row"), "col"),
            P(("groups", "col"), "row"),
            P(("groups", "row"), "col"),
        ),
        check_vma=False,
    )
```

```python
import functools
import math

import jax
import jax.numpy as jnp
from jax import lax
from jax.experimental import pallas as pl
from jax.experimental.pallas import tpu as pltpu
from jax.sharding import PartitionSpec as P

gelu_c = math.sqrt(2.0 / math.pi)
MESH = pl.DeviceIdType.MESH
CHUNK = 512
RING = 8
RELAY, OWN, SPREAD = 1, 3, 6
NT = (((1,), (1,)), ((), ()))
TN = (((0,), (0,)), ((), ()))


def local_gelu(preact, grad_act):
    inner = gelu_c * (preact + 0.044715 * preact * preact * preact)
    tangent = jnp.tanh(inner)
    value = 0.5 * preact * (1.0 + tangent)
    slope = 0.5 * (1.0 + tangent) + 0.5 * preact * (1.0 - tangent * tangent) * gelu_c * (
        1.0 + 3.0 * 0.044715 * preact * preact
    )
    return (value.astype(jnp.bfloat16), (grad_act * slope).astype(jnp.bfloat16))


def block_kernel(
    n_row, n_col, chunks,
    x_ref, dy_ref, win_hbm, wout_hbm,
    acts_hbm, xall_hbm, dyall_hbm, result_ref, gin_ref,
    sums, core_in, chip_out, chip_in, xall, dyall, win, wout, local, outgoing, from_left, from_right, acts,
    w_sem, g_send, g_recv, rs_send, left_recv, right_recv, ag_send, ag_recv, save_sem, tok_sem,
    core_send, core_recv, chip_send, chip_recv,
):
    row, col = lax.axis_index("row"), lax.axis_index("col")
    own = x_ref.shape[0]
    tokens = own * n_row
    pair, core = row // 2, row % 2
    pairs = n_row // 2
    sibling = pair * 2 + 1 - core
    mid = n_col // 2
    has_left = col > 0
    has_right = col < n_col - 1
    edge = jnp.logical_or(col == 0, col == n_col - 1)
    depth = x_ref.shape[1]

    def weight_copies(k):
        at = pl.ds(pl.multiple_of(k * CHUNK, CHUNK), CHUNK)
        return (
            pltpu.make_async_copy(win_hbm.at[:, at], win.at[k], w_sem.at[0, k]),
            pltpu.make_async_copy(wout_hbm.at[at, :], wout.at[k], w_sem.at[1, k]),
        )

    def load(k, carry):
        for copy in weight_copies(k):
            copy.start()
        return carry

    lax.fori_loop(0, chunks, load, 0)

    barrier = pltpu.get_barrier_semaphore()
    pl.semaphore_signal(barrier, inc=1, device_id={"row": sibling}, device_id_type=MESH)
    for o in range(1, pairs):
        peer = lax.rem(pair + o, pairs) * 2 + core
        pl.semaphore_signal(barrier, inc=1, device_id={"row": peer}, device_id_type=MESH)

    @pl.when(has_left)
    def _():
        pl.semaphore_signal(barrier, inc=1, device_id={"col": col - 1}, device_id_type=MESH)

    @pl.when(has_right)
    def _():
        pl.semaphore_signal(barrier, inc=1, device_id={"col": col + 1}, device_id_type=MESH)

    pl.semaphore_wait(barrier, pairs + jnp.where(edge, 1, 2))

    def token_copy(which, block, slot, peer, mine):
        ref, all_ref = ((x_ref, xall), (dy_ref, dyall))[which]
        at = pl.ds(pl.multiple_of(block * own, own), own)
        return pltpu.make_async_remote_copy(
            src_ref=ref if mine else all_ref.at[at],
            dst_ref=all_ref.at[at],
            send_sem=g_send.at[which, slot],
            recv_sem=g_recv.at[which, block],
            device_id={"row": peer},
            device_id_type=MESH,
        )

    sends = []
    for which in range(2):
        for o in range(1, pairs):
            sends.append(token_copy(which, row, o, lax.rem(pair + o, pairs) * 2 + core, True))
            sends[-1].start()
        sends.append(token_copy(which, row, 0, sibling, True))
        sends[-1].start()
    mine = pl.ds(pl.multiple_of(row * own, own), own)
    xall[mine, :] = x_ref[...]
    dyall[mine, :] = dy_ref[...]
    sums[...] = jnp.zeros_like(sums)
    for which in range(2):
        for o in range(1, pairs):
            block = lax.rem(pair + pairs - o, pairs) * 2 + core
            onward = token_copy(which, block, pairs + o - 1, sibling, False)
            onward.wait_recv()
            onward.start()
            sends.append(onward)
    for which in range(2):
        for q in range(pairs):
            token_copy(which, q * 2 + 1 - core, 0, sibling, False).wait_recv()
    for copy in sends:
        copy.wait_send()
    keep = (
        pltpu.make_async_copy(xall, xall_hbm, tok_sem.at[0]),
        pltpu.make_async_copy(dyall, dyall_hbm, tok_sem.at[1]),
    )
    for copy in keep:
        copy.start()

    def owner(k):
        return mid - 1 + lax.rem(k, 2)

    def sum_right(k):
        return pltpu.make_async_remote_copy(
            src_ref=outgoing.at[k], dst_ref=from_left.at[k],
            send_sem=rs_send.at[k], recv_sem=left_recv.at[k],
            device_id={"col": col + 1}, device_id_type=MESH,
        )

    def sum_left(k):
        return pltpu.make_async_remote_copy(
            src_ref=outgoing.at[k], dst_ref=from_right.at[k],
            send_sem=rs_send.at[k], recv_sem=right_recv.at[k],
            device_id={"col": col - 1}, device_id_type=MESH,
        )

    def spread(k, side):
        return pltpu.make_async_remote_copy(
            src_ref=acts.at[k], dst_ref=acts.at[k],
            send_sem=ag_send.at[side, k], recv_sem=ag_recv.at[k],
            device_id={"col": col - 1 + 2 * side}, device_id_type=MESH,
        )

    def save(k):
        return pltpu.make_async_copy(acts.at[k], acts_hbm.at[k], save_sem.at[k])

    def multiply(k):
        for copy in weight_copies(k):
            copy.wait()
        slot = lax.rem(k, RING)
        pre = jnp.dot(xall[...], win[k], preferred_element_type=jnp.float32)
        grad = lax.dot_general(dyall[...], wout[k], NT, preferred_element_type=jnp.float32)

        @pl.when(edge)
        def _():
            outgoing[k, :tokens, :] = pre.astype(jnp.bfloat16)
            outgoing[k, tokens:, :] = grad.astype(jnp.bfloat16)

        @pl.when(jnp.logical_not(edge))
        def _():
            local[slot, :tokens, :] = pre
            local[slot, tokens:, :] = grad

        @pl.when(col == 0)
        def _():
            sum_right(k).start()

        @pl.when(col == n_col - 1)
        def _():
            sum_left(k).start()

    def relay(k):
        slot = lax.rem(k, RING)

        @pl.when(jnp.logical_and(has_left, col < owner(k)))
        def _():
            copy = sum_right(k)
            copy.wait_recv()
            outgoing[k] = (local[slot] + from_left[k].astype(jnp.float32)).astype(jnp.bfloat16)
            copy.start()

        @pl.when(jnp.logical_and(has_right, col > owner(k)))
        def _():
            copy = sum_left(k)
            copy.wait_recv()
            outgoing[k] = (local[slot] + from_right[k].astype(jnp.float32)).astype(jnp.bfloat16)
            copy.start()

    def activate(k):
        slot = lax.rem(k, RING)

        @pl.when(col == owner(k))
        def _():
            sum_right(k).wait_recv()
            sum_left(k).wait_recv()
            total = (
                local[slot] + from_left[k].astype(jnp.float32) + from_right[k].astype(jnp.float32)
            )
            value, slope = local_gelu(total[:tokens], total[tokens:])
            acts[k, :tokens, :] = value
            acts[k, tokens:, :] = slope
            spread(k, 0).start()
            spread(k, 1).start()

    def finish(k):
        @pl.when(col < owner(k))
        def _():
            copy = spread(k, 0)
            copy.wait_recv()

            @pl.when(has_left)
            def _():
                copy.start()

        @pl.when(col > owner(k))
        def _():
            copy = spread(k, 1)
            copy.wait_recv()

            @pl.when(has_right)
            def _():
                copy.start()

        save(k).start()
        sums[0] += jnp.dot(acts[k, :tokens, :], wout[k], preferred_element_type=jnp.float32)
        sums[1] += lax.dot_general(
            acts[k, tokens:, :], win[k], NT, preferred_element_type=jnp.float32
        )

    def step(s, carry):
        for trail, stage in ((0, multiply), (RELAY, relay), (OWN, activate), (SPREAD, finish)):
            @pl.when(jnp.logical_and(s >= trail, s < chunks + trail))
            def _():
                stage(s - trail)
        return carry

    lax.fori_loop(0, chunks + SPREAD, step, 0)

    def rows_of(block):
        return pl.ds(pl.multiple_of(block * own, own), own)

    def to_core(which, o):
        block = lax.rem(pair + o, pairs) * 2 + 1 - core
        return pltpu.make_async_remote_copy(
            src_ref=sums.at[which, rows_of(block)], dst_ref=core_in.at[which, o],
            send_sem=core_send.at[which, o], recv_sem=core_recv.at[which, o],
            device_id={"row": sibling}, device_id_type=MESH,
        )

    def to_chip(which, o):
        return pltpu.make_async_remote_copy(
            src_ref=chip_out.at[which, o], dst_ref=chip_in.at[which, o],
            send_sem=chip_send.at[which, o], recv_sem=chip_recv.at[which, o],
            device_id={"row": lax.rem(pair + o, pairs) * 2 + core}, device_id_type=MESH,
        )

    order = list(range(1, pairs)) + [0]
    for o in order:
        for which in range(2):
            to_core(which, o).start()
    for o in order[:-1]:
        block = lax.rem(pair + o, pairs) * 2 + core
        for which in range(2):
            to_core(which, o).wait_recv()
            chip_out[which, o] = (sums[which, rows_of(block), :] + core_in[which, o]).astype(
                jnp.bfloat16
            )
            to_chip(which, o).start()

    def drain(k, carry):
        @pl.when(col < owner(k))
        def _():
            sum_right(k).wait_send()

        @pl.when(col > owner(k))
        def _():
            sum_left(k).wait_send()

        @pl.when(jnp.logical_and(has_left, col <= owner(k)))
        def _():
            spread(k, 0).wait_send()

        @pl.when(jnp.logical_and(has_right, col >= owner(k)))
        def _():
            spread(k, 1).wait_send()

        save(k).wait()
        return carry

    lax.fori_loop(0, chunks, drain, 0)
    for copy in keep:
        copy.wait()
    for which, ref in ((0, result_ref), (1, gin_ref)):
        to_core(which, 0).wait_recv()
        total = sums[which, rows_of(row), :] + core_in[which, 0]
        for o in range(1, pairs):
            to_chip(which, o).wait_recv()
            total += chip_in[which, o].astype(jnp.float32)
        ref[...] = total.astype(jnp.bfloat16)
    for which in range(2):
        for o in order:
            to_core(which, o).wait_send()
        for o in order[:-1]:
            to_chip(which, o).wait_send()


def run_block(n_row, n_col, x, dy, w_in, w_out):
    own, depth = x.shape
    hidden = w_in.shape[1]
    chunks = hidden // CHUNK
    tokens = own * n_row
    bf, f32 = jnp.bfloat16, jnp.float32
    vmem = pl.BlockSpec(memory_space=pltpu.VMEM)
    anywhere = pl.BlockSpec(memory_space=pl.ANY)
    dma = pltpu.SemaphoreType.DMA
    stack = (chunks, 2 * tokens, CHUNK)
    return pl.pallas_call(
        functools.partial(block_kernel, n_row, n_col, chunks),
        out_shape=(
            jax.ShapeDtypeStruct(stack, bf),
            jax.ShapeDtypeStruct((tokens, depth), bf),
            jax.ShapeDtypeStruct((tokens, depth), bf),
            jax.ShapeDtypeStruct((own, depth), bf),
            jax.ShapeDtypeStruct((own, depth), bf),
        ),
        in_specs=[vmem, vmem, anywhere, anywhere],
        out_specs=(anywhere, anywhere, anywhere, vmem, vmem),
        scratch_shapes=[
            pltpu.VMEM((2, tokens, depth), f32),
            pltpu.VMEM((2, n_row // 2, own, depth), f32),
            pltpu.VMEM((2, n_row // 2, own, depth), bf),
            pltpu.VMEM((2, n_row // 2, own, depth), bf),
            pltpu.VMEM((tokens, depth), bf),
            pltpu.VMEM((tokens, depth), bf),
            pltpu.VMEM((chunks, depth, CHUNK), bf),
            pltpu.VMEM((chunks, CHUNK, depth), bf),
            pltpu.VMEM((RING, 2 * tokens, CHUNK), f32),
            pltpu.VMEM(stack, bf),
            pltpu.VMEM(stack, bf),
            pltpu.VMEM(stack, bf),
            pltpu.VMEM(stack, bf),
            dma((2, chunks)),
            dma((2, n_row)),
            dma((2, n_row)),
            dma((chunks,)),
            dma((chunks,)),
            dma((chunks,)),
            dma((2, chunks)),
            dma((chunks,)),
            dma((chunks,)),
            dma((2,)),
            dma((2, n_row // 2)),
            dma((2, n_row // 2)),
            dma((2, n_row // 2)),
            dma((2, n_row // 2)),
        ],
        compiler_params=pltpu.CompilerParams(
            collective_id=0, has_side_effects=True, vmem_limit_bytes=60 * 2**20
        ),
        cost_estimate=pl.CostEstimate(
            flops=8 * tokens * depth * hidden,
            bytes_accessed=4 * depth * hidden,
            transcendentals=tokens * hidden,
        ),
        name="block",
    )(x, dy, w_in, w_out)


def grads_kernel(x_ref, dy_ref, acts_ref, gin_ref, gout_ref, xt):
    tokens = x_ref.shape[0]

    @pl.when(pl.program_id(0) == 0)
    def _():
        xt[...] = x_ref[...].T

    for i in range(acts_ref.shape[0]):
        at = slice(i * CHUNK, (i + 1) * CHUNK)
        gin_ref[:, at] = jnp.dot(
            xt[...], acts_ref[i, tokens:, :], preferred_element_type=jnp.float32
        ).astype(jnp.bfloat16)
        gout_ref[at, :] = lax.dot_general(
            acts_ref[i, :tokens, :], dy_ref[...], TN, preferred_element_type=jnp.float32
        ).astype(jnp.bfloat16)


def weight_grads(x, dy, acts):
    tokens, depth = x.shape
    chunks = acts.shape[0]
    hidden = chunks * CHUNK
    per = 2
    bf = jnp.bfloat16
    return pl.pallas_call(
        grads_kernel,
        grid=(chunks // per,),
        out_shape=(
            jax.ShapeDtypeStruct((depth, hidden), bf),
            jax.ShapeDtypeStruct((hidden, depth), bf),
        ),
        in_specs=[
            pl.BlockSpec((tokens, depth), lambda s: (0, 0)),
            pl.BlockSpec((tokens, depth), lambda s: (0, 0)),
            pl.BlockSpec((per, 2 * tokens, CHUNK), lambda s: (s, 0, 0)),
        ],
        out_specs=(
            pl.BlockSpec((depth, per * CHUNK), lambda s: (0, s)),
            pl.BlockSpec((per * CHUNK, depth), lambda s: (s, 0)),
        ),
        scratch_shapes=[pltpu.VMEM((depth, tokens), bf)],
        compiler_params=pltpu.CompilerParams(vmem_limit_bytes=60 * 2**20),
        cost_estimate=pl.CostEstimate(
            flops=4 * tokens * depth * hidden,
            bytes_accessed=4 * depth * hidden,
            transcendentals=0,
        ),
        name="grads",
    )(x, dy, acts)


def shards(n_row, n_col, inputs, upstream, weight_in, weight_out):
    acts, x_all, dy_all, result, grad_inputs = run_block(
        n_row, n_col, inputs, upstream, weight_in, weight_out
    )
    grad_weight_in, grad_weight_out = weight_grads(x_all, dy_all, acts)
    return result, grad_inputs, grad_weight_in, grad_weight_out


def solution(mesh):
    placed = (
        P(("groups", "row"), "col"),
        P(("groups", "row"), "col"),
        P("col", "row"),
        P("row", "col"),
    )
    return jax.shard_map(
        functools.partial(shards, mesh.shape["row"], mesh.shape["col"]),
        mesh=mesh,
        in_specs=placed,
        out_specs=(
            P(("groups", "row"), "col"),
            P(("groups", "row"), "col"),
            P(("groups", "col"), "row"),
            P(("groups", "row"), "col"),
        ),
        check_vma=False,
    )
```

```python
import functools
import math

import jax
import jax.numpy as jnp
from jax import lax
from jax.experimental import pallas as pl
from jax.experimental.pallas import tpu as pltpu
from jax.sharding import PartitionSpec as P

gelu_c = math.sqrt(2.0 / math.pi)
MESH = pl.DeviceIdType.MESH
CHUNK = 512
RING = 8
RELAY, OWN, SPREAD = 1, 2, 4
NT = (((1,), (1,)), ((), ()))
TN = (((0,), (0,)), ((), ()))


def local_gelu(preact, grad_act):
    inner = gelu_c * (preact + 0.044715 * preact * preact * preact)
    tangent = jnp.tanh(inner)
    value = 0.5 * preact * (1.0 + tangent)
    slope = 0.5 * (1.0 + tangent) + 0.5 * preact * (1.0 - tangent * tangent) * gelu_c * (
        1.0 + 3.0 * 0.044715 * preact * preact
    )
    return (value.astype(jnp.bfloat16), (grad_act * slope).astype(jnp.bfloat16))


def block_kernel(
    n_row, n_col, chunks,
    x_ref, dy_ref, win_hbm, wout_hbm,
    acts_hbm, xall_hbm, dyall_hbm, result_ref, gin_ref,
    sums, core_in, chip_out, chip_in, xall, dyall, win, wout, local, outgoing, from_left, from_right, acts,
    w_sem, g_send, g_recv, rs_send, left_recv, right_recv, ag_send, ag_recv, save_sem, tok_sem,
    core_send, core_recv, chip_send, chip_recv,
):
    row, col = lax.axis_index("row"), lax.axis_index("col")
    own = x_ref.shape[0]
    tokens = own * n_row
    pair, core = row // 2, row % 2
    pairs = n_row // 2
    sibling = pair * 2 + 1 - core
    mid = n_col // 2
    has_left = col > 0
    has_right = col < n_col - 1
    edge = jnp.logical_or(col == 0, col == n_col - 1)
    depth = x_ref.shape[1]

    def weight_copies(k):
        at = pl.ds(pl.multiple_of(k * CHUNK, CHUNK), CHUNK)
        return (
            pltpu.make_async_copy(win_hbm.at[:, at], win.at[k], w_sem.at[0, k]),
            pltpu.make_async_copy(wout_hbm.at[at, :], wout.at[k], w_sem.at[1, k]),
        )

    def load(k, carry):
        for copy in weight_copies(k):
            copy.start()
        return carry

    lax.fori_loop(0, chunks, load, 0)

    barrier = pltpu.get_barrier_semaphore()
    pl.semaphore_signal(barrier, inc=1, device_id={"row": sibling}, device_id_type=MESH)
    for o in range(1, pairs):
        peer = lax.rem(pair + o, pairs) * 2 + core
        pl.semaphore_signal(barrier, inc=1, device_id={"row": peer}, device_id_type=MESH)

    @pl.when(has_left)
    def _():
        pl.semaphore_signal(barrier, inc=1, device_id={"col": col - 1}, device_id_type=MESH)

    @pl.when(has_right)
    def _():
        pl.semaphore_signal(barrier, inc=1, device_id={"col": col + 1}, device_id_type=MESH)

    pl.semaphore_wait(barrier, pairs + jnp.where(edge, 1, 2))

    def token_copy(which, block, slot, peer, mine):
        ref, all_ref = ((x_ref, xall), (dy_ref, dyall))[which]
        at = pl.ds(pl.multiple_of(block * own, own), own)
        return pltpu.make_async_remote_copy(
            src_ref=ref if mine else all_ref.at[at],
            dst_ref=all_ref.at[at],
            send_sem=g_send.at[which, slot],
            recv_sem=g_recv.at[which, block],
            device_id={"row": peer},
            device_id_type=MESH,
        )

    sends = []
    for which in range(2):
        for o in range(1, pairs):
            sends.append(token_copy(which, row, o, lax.rem(pair + o, pairs) * 2 + core, True))
            sends[-1].start()
        sends.append(token_copy(which, row, 0, sibling, True))
        sends[-1].start()
    mine = pl.ds(pl.multiple_of(row * own, own), own)
    xall[mine, :] = x_ref[...]
    dyall[mine, :] = dy_ref[...]
    sums[...] = jnp.zeros_like(sums)
    for which in range(2):
        for o in range(1, pairs):
            block = lax.rem(pair + pairs - o, pairs) * 2 + core
            onward = token_copy(which, block, pairs + o - 1, sibling, False)
            onward.wait_recv()
            onward.start()
            sends.append(onward)
    for which in range(2):
        for q in range(pairs):
            token_copy(which, q * 2 + 1 - core, 0, sibling, False).wait_recv()
    for copy in sends:
        copy.wait_send()
    keep = (
        pltpu.make_async_copy(xall, xall_hbm, tok_sem.at[0]),
        pltpu.make_async_copy(dyall, dyall_hbm, tok_sem.at[1]),
    )
    for copy in keep:
        copy.start()

    def owner(k):
        return mid - 1 + lax.rem(k, 2)

    def sum_right(k):
        return pltpu.make_async_remote_copy(
            src_ref=outgoing.at[k], dst_ref=from_left.at[k],
            send_sem=rs_send.at[k], recv_sem=left_recv.at[k],
            device_id={"col": col + 1}, device_id_type=MESH,
        )

    def sum_left(k):
        return pltpu.make_async_remote_copy(
            src_ref=outgoing.at[k], dst_ref=from_right.at[k],
            send_sem=rs_send.at[k], recv_sem=right_recv.at[k],
            device_id={"col": col - 1}, device_id_type=MESH,
        )

    def spread(k, side):
        return pltpu.make_async_remote_copy(
            src_ref=acts.at[k], dst_ref=acts.at[k],
            send_sem=ag_send.at[side, k], recv_sem=ag_recv.at[k],
            device_id={"col": col - 1 + 2 * side}, device_id_type=MESH,
        )

    def save(k):
        return pltpu.make_async_copy(acts.at[k], acts_hbm.at[k], save_sem.at[k])

    def multiply(k):
        for copy in weight_copies(k):
            copy.wait()
        slot = lax.rem(k, RING)
        pre = jnp.dot(xall[...], win[k], preferred_element_type=jnp.float32)
        grad = lax.dot_general(dyall[...], wout[k], NT, preferred_element_type=jnp.float32)

        @pl.when(edge)
        def _():
            outgoing[k, :tokens, :] = pre.astype(jnp.bfloat16)
            outgoing[k, tokens:, :] = grad.astype(jnp.bfloat16)

        @pl.when(jnp.logical_not(edge))
        def _():
            local[slot, :tokens, :] = pre
            local[slot, tokens:, :] = grad

        @pl.when(col == 0)
        def _():
            sum_right(k).start()

        @pl.when(col == n_col - 1)
        def _():
            sum_left(k).start()

    def relay(k):
        slot = lax.rem(k, RING)

        @pl.when(jnp.logical_and(has_left, col < owner(k)))
        def _():
            copy = sum_right(k)
            copy.wait_recv()
            outgoing[k] = (local[slot] + from_left[k].astype(jnp.float32)).astype(jnp.bfloat16)
            copy.start()

        @pl.when(jnp.logical_and(has_right, col > owner(k)))
        def _():
            copy = sum_left(k)
            copy.wait_recv()
            outgoing[k] = (local[slot] + from_right[k].astype(jnp.float32)).astype(jnp.bfloat16)
            copy.start()

    def activate(k):
        slot = lax.rem(k, RING)

        @pl.when(col == owner(k))
        def _():
            sum_right(k).wait_recv()
            sum_left(k).wait_recv()
            total = (
                local[slot] + from_left[k].astype(jnp.float32) + from_right[k].astype(jnp.float32)
            )
            value, slope = local_gelu(total[:tokens], total[tokens:])
            acts[k, :tokens, :] = value
            acts[k, tokens:, :] = slope
            spread(k, 0).start()
            spread(k, 1).start()

    def finish(k):
        @pl.when(col < owner(k))
        def _():
            copy = spread(k, 0)
            copy.wait_recv()

            @pl.when(has_left)
            def _():
                copy.start()

        @pl.when(col > owner(k))
        def _():
            copy = spread(k, 1)
            copy.wait_recv()

            @pl.when(has_right)
            def _():
                copy.start()

        save(k).start()
        sums[0] += jnp.dot(acts[k, :tokens, :], wout[k], preferred_element_type=jnp.float32)
        sums[1] += lax.dot_general(
            acts[k, tokens:, :], win[k], NT, preferred_element_type=jnp.float32
        )

    def step(s, carry):
        for trail, stage in ((0, multiply), (RELAY, relay), (OWN, activate), (SPREAD, finish)):
            @pl.when(jnp.logical_and(s >= trail, s < chunks + trail))
            def _():
                stage(s - trail)
        return carry

    lax.fori_loop(0, chunks + SPREAD, step, 0)

    def rows_of(block):
        return pl.ds(pl.multiple_of(block * own, own), own)

    def to_core(which, o):
        block = lax.rem(pair + o, pairs) * 2 + 1 - core
        return pltpu.make_async_remote_copy(
            src_ref=sums.at[which, rows_of(block)], dst_ref=core_in.at[which, o],
            send_sem=core_send.at[which, o], recv_sem=core_recv.at[which, o],
            device_id={"row": sibling}, device_id_type=MESH,
        )

    def to_chip(which, o):
        return pltpu.make_async_remote_copy(
            src_ref=chip_out.at[which, o], dst_ref=chip_in.at[which, o],
            send_sem=chip_send.at[which, o], recv_sem=chip_recv.at[which, o],
            device_id={"row": lax.rem(pair + o, pairs) * 2 + core}, device_id_type=MESH,
        )

    order = list(range(1, pairs)) + [0]
    for o in order:
        for which in range(2):
            to_core(which, o).start()
    for o in order[:-1]:
        block = lax.rem(pair + o, pairs) * 2 + core
        for which in range(2):
            to_core(which, o).wait_recv()
            chip_out[which, o] = (sums[which, rows_of(block), :] + core_in[which, o]).astype(
                jnp.bfloat16
            )
            to_chip(which, o).start()

    def drain(k, carry):
        @pl.when(col < owner(k))
        def _():
            sum_right(k).wait_send()

        @pl.when(col > owner(k))
        def _():
            sum_left(k).wait_send()

        @pl.when(jnp.logical_and(has_left, col <= owner(k)))
        def _():
            spread(k, 0).wait_send()

        @pl.when(jnp.logical_and(has_right, col >= owner(k)))
        def _():
            spread(k, 1).wait_send()

        save(k).wait()
        return carry

    lax.fori_loop(0, chunks, drain, 0)
    for copy in keep:
        copy.wait()
    for which, ref in ((0, result_ref), (1, gin_ref)):
        to_core(which, 0).wait_recv()
        total = sums[which, rows_of(row), :] + core_in[which, 0]
        for o in range(1, pairs):
            to_chip(which, o).wait_recv()
            total += chip_in[which, o].astype(jnp.float32)
        ref[...] = total.astype(jnp.bfloat16)
    for which in range(2):
        for o in order:
            to_core(which, o).wait_send()
        for o in order[:-1]:
            to_chip(which, o).wait_send()


def run_block(n_row, n_col, x, dy, w_in, w_out):
    own, depth = x.shape
    hidden = w_in.shape[1]
    chunks = hidden // CHUNK
    tokens = own * n_row
    bf, f32 = jnp.bfloat16, jnp.float32
    vmem = pl.BlockSpec(memory_space=pltpu.VMEM)
    anywhere = pl.BlockSpec(memory_space=pl.ANY)
    dma = pltpu.SemaphoreType.DMA
    stack = (chunks, 2 * tokens, CHUNK)
    return pl.pallas_call(
        functools.partial(block_kernel, n_row, n_col, chunks),
        out_shape=(
            jax.ShapeDtypeStruct(stack, bf),
            jax.ShapeDtypeStruct((tokens, depth), bf),
            jax.ShapeDtypeStruct((tokens, depth), bf),
            jax.ShapeDtypeStruct((own, depth), bf),
            jax.ShapeDtypeStruct((own, depth), bf),
        ),
        in_specs=[vmem, vmem, anywhere, anywhere],
        out_specs=(anywhere, anywhere, anywhere, vmem, vmem),
        scratch_shapes=[
            pltpu.VMEM((2, tokens, depth), f32),
            pltpu.VMEM((2, n_row // 2, own, depth), f32),
            pltpu.VMEM((2, n_row // 2, own, depth), bf),
            pltpu.VMEM((2, n_row // 2, own, depth), bf),
            pltpu.VMEM((tokens, depth), bf),
            pltpu.VMEM((tokens, depth), bf),
            pltpu.VMEM((chunks, depth, CHUNK), bf),
            pltpu.VMEM((chunks, CHUNK, depth), bf),
            pltpu.VMEM((RING, 2 * tokens, CHUNK), f32),
            pltpu.VMEM(stack, bf),
            pltpu.VMEM(stack, bf),
            pltpu.VMEM(stack, bf),
            pltpu.VMEM(stack, bf),
            dma((2, chunks)),
            dma((2, n_row)),
            dma((2, n_row)),
            dma((chunks,)),
            dma((chunks,)),
            dma((chunks,)),
            dma((2, chunks)),
            dma((chunks,)),
            dma((chunks,)),
            dma((2,)),
            dma((2, n_row // 2)),
            dma((2, n_row // 2)),
            dma((2, n_row // 2)),
            dma((2, n_row // 2)),
        ],
        compiler_params=pltpu.CompilerParams(
            collective_id=0, has_side_effects=True, vmem_limit_bytes=60 * 2**20
        ),
        cost_estimate=pl.CostEstimate(
            flops=8 * tokens * depth * hidden,
            bytes_accessed=4 * depth * hidden,
            transcendentals=tokens * hidden,
        ),
        name="block",
    )(x, dy, w_in, w_out)


def grads_kernel(x_ref, dy_ref, acts_ref, gin_ref, gout_ref, xt):
    tokens = x_ref.shape[0]

    @pl.when(pl.program_id(0) == 0)
    def _():
        xt[...] = x_ref[...].T

    for i in range(acts_ref.shape[0]):
        at = slice(i * CHUNK, (i + 1) * CHUNK)
        gin_ref[:, at] = jnp.dot(
            xt[...], acts_ref[i, tokens:, :], preferred_element_type=jnp.float32
        ).astype(jnp.bfloat16)
        gout_ref[at, :] = lax.dot_general(
            acts_ref[i, :tokens, :], dy_ref[...], TN, preferred_element_type=jnp.float32
        ).astype(jnp.bfloat16)


def weight_grads(x, dy, acts):
    tokens, depth = x.shape
    chunks = acts.shape[0]
    hidden = chunks * CHUNK
    per = 2
    bf = jnp.bfloat16
    return pl.pallas_call(
        grads_kernel,
        grid=(chunks // per,),
        out_shape=(
            jax.ShapeDtypeStruct((depth, hidden), bf),
            jax.ShapeDtypeStruct((hidden, depth), bf),
        ),
        in_specs=[
            pl.BlockSpec((tokens, depth), lambda s: (0, 0)),
            pl.BlockSpec((tokens, depth), lambda s: (0, 0)),
            pl.BlockSpec((per, 2 * tokens, CHUNK), lambda s: (s, 0, 0)),
        ],
        out_specs=(
            pl.BlockSpec((depth, per * CHUNK), lambda s: (0, s)),
            pl.BlockSpec((per * CHUNK, depth), lambda s: (s, 0)),
        ),
        scratch_shapes=[pltpu.VMEM((depth, tokens), bf)],
        compiler_params=pltpu.CompilerParams(vmem_limit_bytes=60 * 2**20),
        cost_estimate=pl.CostEstimate(
            flops=4 * tokens * depth * hidden,
            bytes_accessed=4 * depth * hidden,
            transcendentals=0,
        ),
        name="grads",
    )(x, dy, acts)


def shards(n_row, n_col, inputs, upstream, weight_in, weight_out):
    acts, x_all, dy_all, result, grad_inputs = run_block(
        n_row, n_col, inputs, upstream, weight_in, weight_out
    )
    grad_weight_in, grad_weight_out = weight_grads(x_all, dy_all, acts)
    return result, grad_inputs, grad_weight_in, grad_weight_out


def solution(mesh):
    placed = (
        P(("groups", "row"), "col"),
        P(("groups", "row"), "col"),
        P("col", "row"),
        P("row", "col"),
    )
    return jax.shard_map(
        functools.partial(shards, mesh.shape["row"], mesh.shape["col"]),
        mesh=mesh,
        in_specs=placed,
        out_specs=(
            P(("groups", "row"), "col"),
            P(("groups", "row"), "col"),
            P(("groups", "col"), "row"),
            P(("groups", "row"), "col"),
        ),
        check_vma=False,
    )
```
